32 devices in a mesh: segment: 4 (over x, core), dp: 2 (over y), mp: 4 (over z).
Axes of the slice: x: 2, y: 2, z: 4, core: 2. Of those that a mesh axis runs over, the one named last changes fastest.
Arguments:
- encoder_image_states: bfloat16 [2, 32, 8192], P('dp', 'segment'), may hold values from -6 to 6
- frozen_key_value: bfloat16 [4, 8192, 2, 1024], P('segment', 'dp', None, 'mp'), may hold values from -0.0625 to 0.0625
- adapter_down_weight: bfloat16 [4, 8192, 128], P('segment', 'mp'), may hold values from -0.0625 to 0.0625
- adapter_up_weight: bfloat16 [4, 2, 64, 1024], P('segment', None, None, 'mp'), may hold values from -0.75 to 0.75
- queries: bfloat16 [4, 2, 128, 8192], P('segment', 'dp', None, 'mp'), may hold values from -9 to 9
- cotangent: bfloat16 [4, 2, 128, 8192], P('segment', 'dp', None, 'mp'), may hold values from -1.5 to 1.5
- text_token_length: int32 [2], P('dp'), may hold values from 32 to 128
- image_tile_count: int32 [2], P('dp'), may hold values from 1 to 4
Outputs:
- grad_down: bfloat16 [4, 8192, 128], P('segment', 'mp')
- up_gradient: bfloat16 [4, 2, 64, 1024], P('segment', None, None, 'mp')
- grad_image: float32 [2, 32, 8192], P('dp', 'segment')
The draws below stay inside these ranges and needn't reach their ends.
All inputs are finite; a program needn't handle non-finite values.
Results may differ from the reference program's by a relative error of at most 0.017.
The reference program's roundings to bfloat16 on the way count: a program that leaves them out, or rounds other values in their place, can miss the bound.
Values may be sent and summed in bfloat16 or wider, within the bound.
A program may use at most 64 MiB of HBM per device.

```python
import jax
import jax.numpy as jnp
from jax import lax

MODEL_DIM = 8192
H = 64
HD = 128
TILES = 4
ADAPTER_RANK = 64
TXT = 128
CROSS_LAYERS = 4
SAMPLE_COUNT = 2
IMAGE_TOKENS = 32
KEY_VALUE_COLS = 1024


def draw_queries(key, part):
    base_key = jax.random.fold_in(jax.random.fold_in(key, 7), 0)
    array_shape = (CROSS_LAYERS, SAMPLE_COUNT, TXT, H * HD)
    values = jnp.clip(jax.random.normal(base_key, array_shape, jnp.float32), -5.0, 5.0)
    return values.astype(jnp.bfloat16)


def level_of(key, dims, pieces, smallest, high):
    gain = 1.0
    for axis_at, blocks in pieces:
        heights = jax.random.uniform(jax.random.fold_in(jax.random.fold_in(key, 6), axis_at), (blocks,), jnp.float32, smallest / len(pieces), high / len(pieces))
        gain = gain * jnp.repeat(jnp.exp(heights), dims[axis_at] // blocks).reshape((-1,) + (1,) * (len(dims) - 1 - axis_at))
    return gain


def normal_values(rng, extent, width, bound, cuts=(), kind=jnp.bfloat16):
    result = width * jax.random.normal(rng, extent, jnp.float32)
    if cuts:
        result = result * level_of(rng, extent, cuts, -0.22, 0.18)
    return jnp.clip(result, -bound, bound).astype(kind)


def setup_inputs(seed: int = 0) -> dict:
    key_list = jax.random.split(jax.random.key(seed), 9)
    encoder_image_states = normal_values(key_list[0], (SAMPLE_COUNT, IMAGE_TOKENS, MODEL_DIM), 1.0, 6.0, ((0, 2), (1, 4)))
    frozen_key_value = normal_values(key_list[1], (CROSS_LAYERS, MODEL_DIM, 2, KEY_VALUE_COLS), MODEL_DIM ** -0.5, 0.0625, ((0, 4), (1, 2), (3, 4)))
    adapter_down_weight = normal_values(key_list[2], (CROSS_LAYERS, MODEL_DIM, 2 * ADAPTER_RANK), MODEL_DIM ** -0.5, 0.0625, ((0, 4), (1, 4)))
    adapter_up_weight = normal_values(key_list[3], (CROSS_LAYERS, 2, ADAPTER_RANK, KEY_VALUE_COLS), ADAPTER_RANK ** -0.5, 0.75, ((0, 4), (3, 4)))
    queries = draw_queries(jax.random.fold_in(key_list[8], 71), 0)
    cotangent = normal_values(key_list[5], (CROSS_LAYERS, SAMPLE_COUNT, TXT, H * HD), 0.25, 1.5, ((0, 4), (1, 2), (3, 4)))
    text_token_length = jax.random.randint(key_list[6], (SAMPLE_COUNT,), TXT // 4, TXT + 1).astype(jnp.int32)
    image_tile_count = jax.random.randint(key_list[7], (SAMPLE_COUNT,), 1, TILES + 1).astype(jnp.int32)
    return dict(encoder_image_states=encoder_image_states, frozen_key_value=frozen_key_value, adapter_down_weight=adapter_down_weight, adapter_up_weight=adapter_up_weight, queries=queries, cotangent=cotangent, text_token_length=text_token_length, image_tile_count=image_tile_count)


adapter_scale = 2.0


def layer_terms(image_flat, key_mask, row_mask, frozen, down_proj, up_proj, query_in, cot_in):
    lowrank_state = up_proj.shape[1]
    model_width = frozen.shape[0]
    key_value_columns = frozen.shape[2]
    samples = query_in.shape[0]
    text_rows = query_in.shape[1]
    image_rows = image_flat.shape[0] // samples
    kv_heads = key_value_columns // HD
    group_size = query_in.shape[2] // (HD * kv_heads)
    lowrank_projection = jnp.dot(image_flat, down_proj, preferred_element_type=jnp.float32).astype(jnp.bfloat16)
    adapted_weight = jnp.concatenate([
        jnp.dot(lowrank_projection[:, :lowrank_state], up_proj[0], preferred_element_type=jnp.float32),
        jnp.dot(lowrank_projection[:, lowrank_state:], up_proj[1], preferred_element_type=jnp.float32)], axis=1)
    weight_flat = frozen.reshape(model_width, 2 * key_value_columns)
    frozen_output = jnp.dot(image_flat, weight_flat, preferred_element_type=jnp.float32)
    key_value_pair = (frozen_output + adapter_scale * adapted_weight).astype(jnp.bfloat16)
    key_rows = key_value_pair[:, :key_value_columns].reshape(samples, image_rows, kv_heads, HD).astype(jnp.float32)
    value_rows = key_value_pair[:, key_value_columns:].reshape(samples, image_rows, kv_heads, HD).astype(jnp.float32)
    query_rows = query_in.reshape(samples, text_rows, kv_heads, group_size, HD).astype(jnp.float32)
    cot_rows = cot_in.reshape(samples, text_rows, kv_heads, group_size, HD).astype(jnp.float32)
    scores = jnp.einsum("btgrd,bjgd->bgrtj", query_rows, key_rows) * (HD ** -0.5)
    masked = jnp.where(key_mask[:, None, None, None, :], scores, -1e30)
    row_top = jnp.max(masked, axis=-1, keepdims=True)
    shifted = jnp.exp(masked - row_top)
    attention = shifted / jnp.sum(shifted, axis=-1, keepdims=True)
    row_gate = row_mask[:, None, None, :, None]
    kept = attention.astype(jnp.bfloat16) * row_gate.astype(jnp.bfloat16)
    dweights = jnp.einsum("btgrd,bjgd->bgrtj", cot_rows, value_rows)
    row_delta = jnp.sum(attention * dweights, axis=-1, keepdims=True)
    dscore = (attention * (dweights - row_delta) * row_gate * (HD ** -0.5)).astype(jnp.bfloat16)
    key_grad = jnp.einsum("bgrtj,btgrd->bjgd", dscore.astype(jnp.float32), query_rows)
    value_grad = jnp.einsum("bgrtj,btgrd->bjgd", kept.astype(jnp.float32), cot_rows)
    flat_rows = samples * image_rows
    kv_grad = jnp.concatenate([key_grad.reshape(flat_rows, key_value_columns), value_grad.reshape(flat_rows, key_value_columns)], axis=1).astype(jnp.bfloat16)
    backward_lowrank = (adapter_scale * jnp.concatenate([
        jnp.dot(kv_grad[:, :key_value_columns], up_proj[0].T, preferred_element_type=jnp.float32),
        jnp.dot(kv_grad[:, key_value_columns:], up_proj[1].T, preferred_element_type=jnp.float32)], axis=1)).astype(jnp.bfloat16)
    up_gradient = adapter_scale * jnp.stack([
        jnp.dot(lowrank_projection[:, :lowrank_state].T, kv_grad[:, :key_value_columns], preferred_element_type=jnp.float32),
        jnp.dot(lowrank_projection[:, lowrank_state:].T, kv_grad[:, key_value_columns:], preferred_element_type=jnp.float32)])
    grad_down = jnp.dot(image_flat.T, backward_lowrank, preferred_element_type=jnp.float32)
    grad_img = jnp.dot(kv_grad, weight_flat.T, preferred_element_type=jnp.float32) + jnp.dot(backward_lowrank, down_proj.T, preferred_element_type=jnp.float32)
    return grad_down, up_gradient, grad_img


def reference(encoder_image_states, frozen_key_value, adapter_down_weight, adapter_up_weight, queries, cotangent, text_token_length, image_tile_count):
    image_flat = encoder_image_states.reshape(SAMPLE_COUNT * IMAGE_TOKENS, MODEL_DIM)
    key_mask = jnp.arange(IMAGE_TOKENS, dtype=jnp.int32)[None, :] < (image_tile_count[:, None] * (IMAGE_TOKENS // TILES)).astype(jnp.int32)
    row_mask = (jnp.arange(TXT, dtype=jnp.int32)[None, :] < text_token_length[:, None].astype(jnp.int32)).astype(jnp.float32)

    def accumulate_terms(running_total, layer_in):
        frozen, down_proj, up_proj, query_in, cot_in = layer_in
        grad_down, up_gradient, grad_img = layer_terms(image_flat, key_mask, row_mask, frozen, down_proj, up_proj, query_in, cot_in)
        return running_total + grad_img, (grad_down.astype(jnp.bfloat16), up_gradient.astype(jnp.bfloat16))

    running_total, stacked_layers = lax.scan(accumulate_terms, jnp.zeros((SAMPLE_COUNT * IMAGE_TOKENS, MODEL_DIM), jnp.float32), (frozen_key_value, adapter_down_weight, adapter_up_weight, queries, cotangent))
    return stacked_layers[0], stacked_layers[1], running_total.reshape(SAMPLE_COUNT, IMAGE_TOKENS, MODEL_DIM)
```

```python
import functools

import jax
import jax.numpy as jnp
from jax import lax
from jax.experimental import pallas as pl
from jax.experimental.pallas import tpu as pltpu
from jax.sharding import PartitionSpec as P

HD = 128
TILES = 4
ADAPTER_SCALE = 2.0
F32 = jnp.float32
BF16 = jnp.bfloat16
NN = (((1,), (0,)), ((), ()))
NT = (((1,), (1,)), ((), ()))
TN = (((0,), (0,)), ((), ()))


def dot(a, b, dims):
    return lax.dot_general(a, b, dims, preferred_element_type=F32)


def flip(index, bit):
    return index + bit - 2 * bit * lax.rem(lax.div(index, bit), 2)


def bits_down(n):
    bits = []
    while n > 1:
        n //= 2
        bits.append(n)
    return bits


def kernel(
    sizes,
    len_ref, tiles_ref, img_ref, up_ref, w_hbm, a_hbm, q_hbm, c_hbm,
    gdown_ref, gup_ref, gimg_ref,
    w, a, q, c, x, xh, low_p, low_r, kv_p, kv_r, dkv_own, dkv, back_p, back_r,
    g, zs, zr, fin, fr, load_sem, send_sem, recv_sem, *halves,
):
    S, D, M = sizes
    s, d, m = lax.axis_index("segment"), lax.axis_index("dp"), lax.axis_index("mp")
    rows_loc, width = img_ref.shape
    nb = S * D
    rows = nb * rows_loc
    srows = S * rows_loc
    cw = w.shape[0]
    kvc = w.shape[1] // 2
    qw = a.shape[0]
    zw = cw // M
    s_bits, d_bits = bits_down(S), bits_down(D)

    loads = [
        pltpu.make_async_copy(src, dst, load_sem.at[i])
        for i, (src, dst) in enumerate([(w_hbm, w), (a_hbm, a), (q_hbm, q), (c_hbm, c)])
    ]
    for load in loads:
        load.start()

    barrier = pltpu.get_barrier_semaphore()
    peers = [(flip(s, b), d, m) for b in s_bits]
    for i in range(D):
        for j in range(M):
            if i or j:
                peers.append((s, lax.rem(d + i, D), lax.rem(m + j, M)))
    for peer in peers:
        pl.semaphore_signal(barrier, inc=1, device_id=peer, device_id_type=pl.DeviceIdType.MESH)
    pl.semaphore_wait(barrier, len(peers))

    started = []

    def send(src, dst, peer):
        k = len(started)
        copy = pltpu.make_async_remote_copy(
            src_ref=src, dst_ref=dst, send_sem=send_sem.at[k], recv_sem=recv_sem.at[k],
            device_id=peer, device_id_type=pl.DeviceIdType.MESH,
        )
        copy.start()
        started.append(copy)
        return copy

    steps = [("d", b) for b in d_bits] + [("s", b) for b in s_bits]

    def across(step, at):
        kind, b = step
        return (at[0], flip(at[1], b)) if kind == "d" else (flip(at[0], b), at[1])

    me = (s, d)
    held = [[] for _ in steps]
    for k, step in enumerate(steps):
        to = across(step, me)
        held[k].append((send(img_ref, x.at[d * S + s], (*to, m)), across(step, me)))
    x[d * S + s] = img_ref[...]
    for k in range(len(steps)):
        for copy, at in list(held[k]):
            copy.wait_recv()
            slot = x.at[at[1] * S + at[0]]
            for later in range(k + 1, len(steps)):
                to = across(steps[later], me)
                held[later].append((send(slot, slot, (*to, m)), across(steps[later], at)))

    ukk = jnp.concatenate([up_ref[0], jnp.zeros_like(up_ref[0])], axis=0)
    uvv = jnp.concatenate([jnp.zeros_like(up_ref[1]), up_ref[1]], axis=0)

    loads[1].wait()
    xq = x[:, :, pl.ds(pl.multiple_of(m * qw, 128), qw)].astype(F32).reshape(rows, qw).astype(BF16)
    low_p[...] = dot(xq, a[...], NN)
    low_c = [
        send(low_p, low_r.at[m], (s, d, lax.rem(m + j, M))) for j in range(1, M)
    ]
    low_r[m] = low_p[...]

    xh[...] = (
        x[:, :, pl.ds(pl.multiple_of(d * cw, 128), cw)].astype(F32).reshape(rows, cw).astype(BF16)
    )
    loads[0].wait()
    kv_p[...] = dot(xh[...], w[...], NN).reshape(kv_p.shape)
    kv_c = [
        send(kv_p.at[lax.rem(d + i, D)], kv_r.at[d], (s, lax.rem(d + i, D), m))
        for i in range(1, D)
    ]
    kv_r[d] = kv_p[d]
    for copy in low_c:
        copy.wait_recv()
    low = jnp.sum(low_r[...], axis=0).astype(BF16)
    fin_low = low.astype(F32).reshape(D, srows, low.shape[1])
    low_own = jnp.zeros((srows, low.shape[1]), F32)
    for i in range(D):
        low_own = jnp.where(d == i, fin_low[i], low_own)
    low_own = low_own.astype(BF16)
    adapted = jnp.concatenate([dot(low_own, ukk, NN), dot(low_own, uvv, NN)], axis=1)
    for copy in kv_c:
        copy.wait_recv()
    kv = (jnp.sum(kv_r[...], axis=0) + ADAPTER_SCALE * adapted).astype(BF16)

    loads[2].wait()
    loads[3].wait()
    text = q.shape[0]
    heads = q.shape[1] // HD
    kv_heads = kvc // HD
    group = heads // kv_heads
    cols = group * text
    live = (
        lax.rem(lax.broadcasted_iota(jnp.int32, (1, cols), 1), text) < len_ref[0]
    ).astype(F32)
    valid = lax.broadcasted_iota(jnp.int32, (srows, 1), 0) < tiles_ref[0] * (srows // TILES)
    for h in range(kv_heads):
        qs = jnp.concatenate(
            [q[:, (h * group + r) * HD : (h * group + r + 1) * HD] for r in range(group)], axis=0
        )
        cs = jnp.concatenate(
            [c[:, (h * group + r) * HD : (h * group + r + 1) * HD] for r in range(group)], axis=0
        )
        keys = kv[:, h * HD : (h + 1) * HD]
        vals = kv[:, kvc + h * HD : kvc + (h + 1) * HD]
        scores = jnp.where(valid, dot(keys, qs, NT) * HD ** (-0.5), -1e30)
        shifted = jnp.exp(scores - jnp.max(scores, axis=0, keepdims=True))
        att = shifted / jnp.sum(shifted, axis=0, keepdims=True)
        kept = (att.astype(BF16).astype(F32) * live).astype(BF16)
        dp = dot(vals, cs, NT)
        delta = jnp.sum(att * dp, axis=0, keepdims=True)
        ds = (att * (dp - delta) * live * HD ** (-0.5)).astype(BF16)
        dkv_own[:, h * HD : (h + 1) * HD] = dot(ds, qs, NN).astype(BF16)
        dkv_own[:, kvc + h * HD : kvc + (h + 1) * HD] = dot(kept, cs, NN).astype(BF16)

    dkv_c = [
        send(dkv_own, dkv.at[d], (s, lax.rem(d + i, D), m)) for i in range(1, D)
    ]
    dkv[d] = dkv_own[...]
    for copy in dkv_c:
        copy.wait_recv()
    dall = dkv[...].reshape(rows, 2 * kvc)

    back_p[...] = ADAPTER_SCALE * (dot(dall[:, :kvc], ukk, NT) + dot(dall[:, kvc:], uvv, NT))
    back_c = [
        send(back_p, back_r.at[m], (s, d, lax.rem(m + j, M))) for j in range(1, M)
    ]
    back_r[m] = back_p[...]

    step = min(cw, 1024)
    for j in range(0, cw, step):
        g[:, :, j : j + step] = dot(dall, w[j : j + step, :], NT).reshape(nb, rows_loc, step)

    for copy in back_c:
        copy.wait_recv()
    back = jnp.sum(back_r[...], axis=0).astype(BF16)

    if cw >= qw:
        @pl.when(lax.div(m, cw // qw) == d)
        def _():
            at = pl.ds(pl.multiple_of(lax.rem(m, cw // qw) * qw, 128), qw)
            g[:, :, at] = g[:, :, at] + dot(back, a[...], NT).reshape(nb, rows_loc, qw)
    else:
        @pl.when(lax.div(d, qw // cw) == m)
        def _():
            at = pl.ds(pl.multiple_of(lax.rem(d, qw // cw) * cw, 128), cw)
            g[...] = g[...] + dot(back, a[at, :], NT).reshape(nb, rows_loc, cw)


    def adapters():
        up = jnp.concatenate(
            [
                dot(low, dall[:, :kvc], TN)[: low.shape[1] // 2],
                dot(low, dall[:, kvc:], TN)[low.shape[1] // 2 :],
            ],
            axis=0,
        )
        gup_ref[...] = (ADAPTER_SCALE * up).astype(BF16).reshape(gup_ref.shape)

    def down():
        xq2 = (
            x[:, :, pl.ds(pl.multiple_of(m * qw, 128), qw)]
            .astype(F32).reshape(rows, qw).astype(BF16)
        )
        gdown_ref[...] = dot(xq2, back, TN).astype(BF16)

    beside = [adapters, down]
    for n, b in enumerate(reversed(s_bits)):
        out_buf, in_buf = halves[2 * n], halves[2 * n + 1]
        count = S // (2 * b)
        mine = lax.rem(lax.div(s, b), 2)
        base = lax.rem(s, b)
        for i in range(D):
            for t in range(count):
                at = i * S + base + b * (1 - mine) + 2 * b * t
                out_buf[i * count + t] = g[at].astype(BF16)
        copy = send(out_buf, in_buf, (flip(s, b), d, m))
        if beside:
            beside.pop(0)()
        copy.wait_recv()
        for i in range(D):
            for t in range(count):
                at = i * S + base + b * mine + 2 * b * t
                g[at] = g[at] + in_buf[i * count + t].astype(F32)
    for work in beside:
        work()

    for j in range(1, M):
        to = lax.rem(m + j, M)
        for i in range(D):
            zs[j - 1, i] = g[i * S + s, :, pl.ds(pl.multiple_of(to * zw, 128), zw)].astype(BF16)
    z_c = [
        send(zs.at[j - 1], zr.at[j - 1], (s, d, lax.rem(m + j, M))) for j in range(1, M)
    ]
    for copy in z_c:
        copy.wait_recv()
    for i in range(D):
        total = g[i * S + s, :, pl.ds(pl.multiple_of(m * zw, 128), zw)]
        for j in range(M - 1):
            total = total + zr[j, i].astype(F32)
        fin[i] = total.astype(BF16)
    f_c = []
    for i in range(D):
        for j in range(M):
            if i or j:
                to = lax.rem(d + i, D)
                f_c.append(send(fin.at[to], fr.at[d * M + m], (s, to, lax.rem(m + j, M))))
    fr[d * M + m] = fin[d]
    for copy in f_c:
        copy.wait_recv()
    for i in range(D * M):
        gimg_ref[:, i * zw : (i + 1) * zw] = fr[i].astype(F32)
    for copy in started:
        copy.wait_send()


def body(
    encoder_image_states,
    frozen_key_value,
    adapter_down_weight,
    adapter_up_weight,
    queries,
    cotangent,
    text_token_length,
    image_tile_count,
    *,
    sizes,
):
    S, D, M = sizes
    rows_loc, width = encoder_image_states.shape[1:]
    cw, kvc = frozen_key_value.shape[1], frozen_key_value.shape[3]
    qw, ranks = adapter_down_weight.shape[1:]
    text, qcols = queries.shape[2:]
    nb = S * D
    rows, srows = nb * rows_loc, S * rows_loc
    zw = cw // M
    vmem = pl.BlockSpec(memory_space=pltpu.VMEM)
    smem = pl.BlockSpec(memory_space=pltpu.SMEM)
    hbm = pl.BlockSpec(memory_space=pl.ANY)
    halves = []
    bits = bits_down(S)
    for b in reversed(bits):
        halves += [pltpu.VMEM((D * S // (2 * b), rows_loc, cw), BF16)] * 2
    sends = (nb - 1) + 3 * (M - 1) + 2 * (D - 1) + len(bits) + (D * M - 1)
    down, up, image = pl.pallas_call(
        functools.partial(kernel, sizes),
        out_shape=(
            jax.ShapeDtypeStruct((qw, ranks), BF16),
            jax.ShapeDtypeStruct(adapter_up_weight.shape[1:], BF16),
            jax.ShapeDtypeStruct((rows_loc, width), F32),
        ),
        in_specs=[smem, smem, vmem, vmem, hbm, hbm, hbm, hbm],
        out_specs=(vmem, vmem, vmem),
        scratch_shapes=[
            pltpu.VMEM((cw, 2 * kvc), BF16),
            pltpu.VMEM((qw, ranks), BF16),
            pltpu.VMEM((text, qcols), BF16),
            pltpu.VMEM((text, qcols), BF16),
            pltpu.VMEM((nb, rows_loc, width), BF16),
            pltpu.VMEM((rows, cw), BF16),
            pltpu.VMEM((rows, ranks), F32),
            pltpu.VMEM((M, rows, ranks), F32),
            pltpu.VMEM((D, srows, 2 * kvc), F32),
            pltpu.VMEM((D, srows, 2 * kvc), F32),
            pltpu.VMEM((srows, 2 * kvc), BF16),
            pltpu.VMEM((D, srows, 2 * kvc), BF16),
            pltpu.VMEM((rows, ranks), F32),
            pltpu.VMEM((M, rows, ranks), F32),
            pltpu.VMEM((nb, rows_loc, cw), F32),
            pltpu.VMEM((M - 1, D, rows_loc, zw), BF16),
            pltpu.VMEM((M - 1, D, rows_loc, zw), BF16),
            pltpu.VMEM((D, rows_loc, zw), BF16),
            pltpu.VMEM((D * M, rows_loc, zw), BF16),
            pltpu.SemaphoreType.DMA((4,)),
            pltpu.SemaphoreType.DMA((sends,)),
            pltpu.SemaphoreType.DMA((sends,)),
            *halves,
        ],
        compiler_params=pltpu.CompilerParams(
            collective_id=0, has_side_effects=True, vmem_limit_bytes=58 * 2**20
        ),
    )(
        text_token_length,
        image_tile_count,
        encoder_image_states[0],
        adapter_up_weight[0],
        frozen_key_value[0].reshape(cw, 2 * kvc),
        adapter_down_weight[0],
        queries[0, 0],
        cotangent[0, 0],
    )
    return down[None], up[None], image[None]


def solution(mesh):
    in_specs = (
        P("dp", "segment", None),
        P("segment", "dp", None, "mp"),
        P("segment", "mp", None),
        P("segment", None, None, "mp"),
        P("segment", "dp", None, "mp"),
        P("segment", "dp", None, "mp"),
        P("dp"),
        P("dp"),
    )
    out_specs = (P("segment", "mp", None), P("segment", None, None, "mp"), P("dp", "segment", None))
    sizes = (mesh.shape["segment"], mesh.shape["dp"], mesh.shape["mp"])
    return jax.shard_map(
        functools.partial(body, sizes=sizes),
        mesh=mesh, in_specs=in_specs, out_specs=out_specs, check_vma=False,
    )
```

```python
import functools

import jax
import jax.numpy as jnp
from jax import lax
from jax.experimental import pallas as pl
from jax.experimental.pallas import tpu as pltpu
from jax.sharding import PartitionSpec as P

HD = 128
TILES = 4
ADAPTER_SCALE = 2.0
F32 = jnp.float32
BF16 = jnp.bfloat16
NN = (((1,), (0,)), ((), ()))
NT = (((1,), (1,)), ((), ()))
TN = (((0,), (0,)), ((), ()))


def dot(a, b, dims):
    return lax.dot_general(a, b, dims, preferred_element_type=F32)


def flip(index, bit):
    return index + bit - 2 * bit * lax.rem(lax.div(index, bit), 2)


def bits_down(n):
    bits = []
    while n > 1:
        n //= 2
        bits.append(n)
    return bits


def kernel(
    sizes, parts,
    len_ref, tiles_ref, img_ref, up_ref, w_hbm, a_hbm, q_hbm, c_hbm,
    gdown_ref, gup_ref, gimg_ref,
    w, a, q, c, xh, xq, low_p, low_r, low_b, kv_p, kv_r, dkv_own, dkv, back_p, back_r,
    g, zs, zr, fin, fr, load_sem, send_sem, recv_sem, *halves,
):
    S, D, M = sizes
    s, d, m = lax.axis_index("segment"), lax.axis_index("dp"), lax.axis_index("mp")
    rows_loc = xh.shape[1]
    nb = S * D
    rows = nb * rows_loc
    srows = S * rows_loc
    cw = w.shape[0]
    kvc = w.shape[1] // 2
    qw = a.shape[0]
    pw = cw // parts
    zw = pw // M
    s_bits, d_bits = bits_down(S), bits_down(D)

    def columns(at, size):
        return pl.ds(pl.multiple_of(at, 128), size)

    loads = [
        pltpu.make_async_copy(src, dst, load_sem.at[i])
        for i, (src, dst) in enumerate(
            [
                (img_ref.at[:, columns(d * cw, cw)], xh.at[d * S + s]),
                (img_ref.at[:, columns(m * qw, qw)], xq.at[d, s]),
                (a_hbm, a),
                (w_hbm, w),
                (q_hbm, q),
                (c_hbm, c),
            ]
        )
    ]
    for load in loads:
        load.start()

    others = [(i, j) for i in range(D) for j in range(M) if i or j]
    barrier = pltpu.get_barrier_semaphore()
    peers = [(flip(s, b), d, m) for b in s_bits]
    peers += [(s, lax.rem(d + i, D), lax.rem(m + j, M)) for i, j in others]
    for peer in peers:
        pl.semaphore_signal(barrier, inc=1, device_id=peer, device_id_type=pl.DeviceIdType.MESH)
    pl.semaphore_wait(barrier, len(peers))

    started = []

    def send(src, dst, peer):
        k = len(started)
        copy = pltpu.make_async_remote_copy(
            src_ref=src, dst_ref=dst, send_sem=send_sem.at[k], recv_sem=recv_sem.at[k],
            device_id=peer, device_id_type=pl.DeviceIdType.MESH,
        )
        copy.start()
        started.append(copy)
        return copy

    steps = [("d", b) for b in d_bits] + [("s", b) for b in s_bits]

    def across(step, at):
        kind, b = step
        return (at[0], flip(at[1], b)) if kind == "d" else (flip(at[0], b), at[1])

    me = (s, d)
    held = [[] for _ in steps]
    for k, step in enumerate(steps):
        to = across(step, me)
        half = img_ref.at[:, columns(to[1] * cw, cw)]
        held[k].append((send(half, xh.at[d * S + s], (*to, m)), "half", to))
        if step[0] == "s":
            quarter = img_ref.at[:, columns(m * qw, qw)]
            held[k].append((send(quarter, xq.at[d, s], (*to, m)), "quarter", to))
    for k in range(len(steps)):
        for copy, kind, at in list(held[k]):
            copy.wait_recv()
            slot = xh.at[at[1] * S + at[0]] if kind == "half" else xq.at[d, at[0]]
            for later in range(k + 1, len(steps)):
                to = across(steps[later], me)
                held[later].append(
                    (send(slot, slot, (*to, m)), kind, across(steps[later], at))
                )

    ukk = jnp.concatenate([up_ref[0], jnp.zeros_like(up_ref[0])], axis=0)
    uvv = jnp.concatenate([jnp.zeros_like(up_ref[1]), up_ref[1]], axis=0)

    loads[0].wait()
    loads[1].wait()
    loads[2].wait()
    mine_q = xq[d].astype(F32).reshape(srows, qw).astype(BF16)
    low_p[...] = dot(mine_q, a[...], NN)
    low_c = [send(low_p, low_r.at[m], (s, d, lax.rem(m + j, M))) for j in range(1, M)]
    low_r[m] = low_p[...]

    xall = xh[...].astype(F32).reshape(rows, cw).astype(BF16)
    loads[3].wait()
    kv_p[...] = dot(xall, w[...], NN).reshape(kv_p.shape)
    samples = [lax.rem(d + i, D) for i in range(1, D)]
    kv_c = [send(kv_p.at[to], kv_r.at[d], (s, to, m)) for to in samples]
    xq_c = [send(xq.at[d], xq.at[d], (s, to, m)) for to in samples]
    kv_r[d] = kv_p[d]
    for copy in low_c:
        copy.wait_recv()
    low_own = jnp.sum(low_r[...], axis=0).astype(BF16)
    low_b[d] = low_own
    lowb_c = [send(low_b.at[d], low_b.at[d], (s, to, m)) for to in samples]
    adapted = jnp.concatenate([dot(low_own, ukk, NN), dot(low_own, uvv, NN)], axis=1)
    for copy in kv_c:
        copy.wait_recv()
    kv = (jnp.sum(kv_r[...], axis=0) + ADAPTER_SCALE * adapted).astype(BF16)

    loads[4].wait()
    loads[5].wait()
    text = q.shape[0]
    heads = q.shape[1] // HD
    kv_heads = kvc // HD
    group = heads // kv_heads
    cols = group * text
    live = (
        lax.rem(lax.broadcasted_iota(jnp.int32, (1, cols), 1), text) < len_ref[0]
    ).astype(F32)
    valid = lax.broadcasted_iota(jnp.int32, (srows, 1), 0) < tiles_ref[0] * (srows // TILES)
    for h in range(kv_heads):
        qs = jnp.concatenate(
            [q[:, (h * group + r) * HD : (h * group + r + 1) * HD] for r in range(group)], axis=0
        )
        cs = jnp.concatenate(
            [c[:, (h * group + r) * HD : (h * group + r + 1) * HD] for r in range(group)], axis=0
        )
        keys = kv[:, h * HD : (h + 1) * HD]
        vals = kv[:, kvc + h * HD : kvc + (h + 1) * HD]
        scores = jnp.where(valid, dot(keys, qs, NT) * HD ** (-0.5), -1e30)
        shifted = jnp.exp(scores - jnp.max(scores, axis=0, keepdims=True))
        att = shifted / jnp.sum(shifted, axis=0, keepdims=True)
        kept = (att.astype(BF16).astype(F32) * live).astype(BF16)
        dp = dot(vals, cs, NT)
        delta = jnp.sum(att * dp, axis=0, keepdims=True)
        ds = (att * (dp - delta) * live * HD ** (-0.5)).astype(BF16)
        dkv_own[:, h * HD : (h + 1) * HD] = dot(ds, qs, NN).astype(BF16)
        dkv_own[:, kvc + h * HD : kvc + (h + 1) * HD] = dot(kept, cs, NN).astype(BF16)

    dkv_c = [send(dkv_own, dkv.at[d], (s, to, m)) for to in samples]
    own = dkv_own[...]
    dkv[d] = own
    back_p[...] = ADAPTER_SCALE * (dot(own[:, :kvc], ukk, NT) + dot(own[:, kvc:], uvv, NT))
    back_c = [
        send(back_p, back_r.at[d, m], (s, lax.rem(d + i, D), lax.rem(m + j, M)))
        for i, j in others
    ]
    back_r[d, m] = back_p[...]
    for copy in dkv_c:
        copy.wait_recv()
    dall = dkv[...].reshape(rows, 2 * kvc)

    step = min(cw, 1024)
    for j in range(0, cw, step):
        g[:, :, j : j + step] = dot(dall, w[j : j + step, :], NT).reshape(nb, rows_loc, step)

    for copy in back_c:
        copy.wait_recv()
    back = jnp.sum(back_r[...], axis=1).reshape(rows, back_r.shape[3]).astype(BF16)

    if cw >= qw:
        @pl.when(lax.div(m, cw // qw) == d)
        def _():
            at = columns(lax.rem(m, cw // qw) * qw, qw)
            g[:, :, at] = g[:, :, at] + dot(back, a[...], NT).reshape(nb, rows_loc, qw)
    else:
        @pl.when(lax.div(d, qw // cw) == m)
        def _():
            at = columns(lax.rem(d, qw // cw) * cw, cw)
            g[...] = g[...] + dot(back, a[at, :], NT).reshape(nb, rows_loc, cw)

    def adapter_up():
        for copy in lowb_c:
            copy.wait_recv()
        low = low_b[...].reshape(rows, low_b.shape[2])
        rank = low.shape[1] // 2
        gup_ref[0] = (ADAPTER_SCALE * dot(low, dall[:, :kvc], TN)[:rank]).astype(BF16)
        gup_ref[1] = (ADAPTER_SCALE * dot(low, dall[:, kvc:], TN)[rank:]).astype(BF16)

    def adapter_down():
        for copy in xq_c:
            copy.wait_recv()
        all_q = xq[...].astype(F32).reshape(rows, qw).astype(BF16)
        gdown_ref[...] = dot(all_q, back, TN).astype(BF16)

    ladder = list(reversed(s_bits))
    flying = {}

    def halve_send(n, p):
        b = ladder[n]
        count = S // (2 * b)
        theirs = lax.rem(s, b) + b * (1 - lax.rem(lax.div(s, b), 2))
        for i in range(D):
            for t in range(count):
                halves[2 * n][p, i * count + t] = g[
                    i * S + theirs + 2 * b * t, :, p * pw : (p + 1) * pw
                ].astype(BF16)
        flying[p] = [send(halves[2 * n].at[p], halves[2 * n + 1].at[p], (flip(s, b), d, m))]

    def halve_take(n, p):
        b = ladder[n]
        count = S // (2 * b)
        ours = lax.rem(s, b) + b * lax.rem(lax.div(s, b), 2)
        flying[p][0].wait_recv()
        for i in range(D):
            for t in range(count):
                at = i * S + ours + 2 * b * t
                g[at, :, p * pw : (p + 1) * pw] = g[at, :, p * pw : (p + 1) * pw] + halves[
                    2 * n + 1
                ][p, i * count + t].astype(F32)

    def group_send(p):
        for j in range(1, M):
            to = lax.rem(m + j, M)
            for i in range(D):
                zs[p, j - 1, i] = g[i * S + s, :, columns(p * pw + to * zw, zw)].astype(BF16)
        flying[p] = [
            send(zs.at[p, j - 1], zr.at[p, j - 1], (s, d, lax.rem(m + j, M)))
            for j in range(1, M)
        ]

    def group_take(p):
        for copy in flying[p]:
            copy.wait_recv()
        for i in range(D):
            total = g[i * S + s, :, columns(p * pw + m * zw, zw)]
            for j in range(M - 1):
                total = total + zr[p, j, i].astype(F32)
            fin[p, i] = total.astype(BF16)
        flying[p] = []
        for i, j in others:
            to = lax.rem(d + i, D)
            flying[p].append(
                send(fin.at[p, to], fr.at[p, d * M + m], (s, to, lax.rem(m + j, M)))
            )
        fr[p, d * M + m] = fin[p, d]

    def finish(p):
        for copy in flying[p]:
            copy.wait_recv()
        for i in range(D):
            for j in range(M):
                at = i * cw + p * pw + j * zw
                gimg_ref[:, at : at + zw] = fr[p, i * M + j].astype(F32)

    for p in range(parts):
        halve_send(0, p)
    adapter_up()
    stages = []
    for n in range(1, len(ladder)):
        stages.append(lambda p, n=n: (halve_take(n - 1, p), halve_send(n, p)))
    stages.append(lambda p: (halve_take(len(ladder) - 1, p), group_send(p)))
    stages.append(group_take)
    stages.append(finish)
    for t in range(parts + len(stages) - 1):
        for k, stage in enumerate(stages):
            if 0 <= t - k < parts:
                stage(t - k)
        if t == parts - 1:
            adapter_down()
    for copy in started:
        copy.wait_send()


def deliver(x0, x1, x2, y0, y1, y2, sems):
    copies = [
        pltpu.make_async_copy(x, y, sems.at[i])
        for i, (x, y) in enumerate([(x0, y0), (x1, y1), (x2, y2)])
    ]
    for copy in copies:
        copy.start()
    for copy in copies:
        copy.wait()


def body(
    encoder_image_states,
    frozen_key_value,
    adapter_down_weight,
    adapter_up_weight,
    queries,
    cotangent,
    text_token_length,
    image_tile_count,
    *,
    sizes,
):
    S, D, M = sizes
    rows_loc, width = encoder_image_states.shape[1:]
    cw, kvc = frozen_key_value.shape[1], frozen_key_value.shape[3]
    qw, ranks = adapter_down_weight.shape[1:]
    text, qcols = queries.shape[2:]
    nb = S * D
    rows, srows = nb * rows_loc, S * rows_loc
    parts = max(1, min(2, cw // M // 128))
    pw = cw // parts
    zw = pw // M
    vmem = pl.BlockSpec(memory_space=pltpu.VMEM)
    smem = pl.BlockSpec(memory_space=pltpu.SMEM)
    hbm = pl.BlockSpec(memory_space=pl.ANY)
    halves = []
    bits = bits_down(S)
    for b in reversed(bits):
        halves += [pltpu.VMEM((parts, D * S // (2 * b), rows_loc, pw), BF16)] * 2
    sends = (nb - 1) + (S - 1) + (M - 1) + 4 * (D - 1) + (D * M - 1)
    sends += parts * (len(bits) + (M - 1) + (D * M - 1))
    shapes = (
        jax.ShapeDtypeStruct((qw, ranks), BF16),
        jax.ShapeDtypeStruct(adapter_up_weight.shape[1:], BF16),
        jax.ShapeDtypeStruct((rows_loc, width), F32),
    )
    down, up, image = pl.pallas_call(
        functools.partial(kernel, sizes, parts),
        out_shape=shapes,
        in_specs=[smem, smem, hbm, vmem, hbm, hbm, hbm, hbm],
        out_specs=(vmem, vmem, vmem),
        scratch_shapes=[
            pltpu.VMEM((cw, 2 * kvc), BF16),
            pltpu.VMEM((qw, ranks), BF16),
            pltpu.VMEM((text, qcols), BF16),
            pltpu.VMEM((text, qcols), BF16),
            pltpu.VMEM((nb, rows_loc, cw), BF16),
            pltpu.VMEM((D, S, rows_loc, qw), BF16),
            pltpu.VMEM((srows, ranks), F32),
            pltpu.VMEM((M, srows, ranks), F32),
            pltpu.VMEM((D, srows, ranks), BF16),
            pltpu.VMEM((D, srows, 2 * kvc), F32),
            pltpu.VMEM((D, srows, 2 * kvc), F32),
            pltpu.VMEM((srows, 2 * kvc), BF16),
            pltpu.VMEM((D, srows, 2 * kvc), BF16),
            pltpu.VMEM((srows, ranks), F32),
            pltpu.VMEM((D, M, srows, ranks), F32),
            pltpu.VMEM((nb, rows_loc, cw), F32),
            pltpu.VMEM((parts, M - 1, D, rows_loc, zw), BF16),
            pltpu.VMEM((parts, M - 1, D, rows_loc, zw), BF16),
            pltpu.VMEM((parts, D, rows_loc, zw), BF16),
            pltpu.VMEM((parts, D * M, rows_loc, zw), BF16),
            pltpu.SemaphoreType.DMA((6,)),
            pltpu.SemaphoreType.DMA((sends,)),
            pltpu.SemaphoreType.DMA((sends,)),
            *halves,
        ],
        compiler_params=pltpu.CompilerParams(
            collective_id=0, has_side_effects=True, vmem_limit_bytes=58 * 2**20
        ),
    )(
        text_token_length,
        image_tile_count,
        encoder_image_states[0],
        adapter_up_weight[0],
        frozen_key_value[0].reshape(cw, 2 * kvc),
        adapter_down_weight[0],
        queries[0, 0],
        cotangent[0, 0],
    )
    down, up, image = pl.pallas_call(
        deliver,
        out_shape=shapes,
        in_specs=[hbm] * 3,
        out_specs=(hbm,) * 3,
        scratch_shapes=[pltpu.SemaphoreType.DMA((3,))],
        compiler_params=pltpu.CompilerParams(vmem_limit_bytes=58 * 2**20),
    )(down, up, image)
    return down[None], up[None], image[None]


def solution(mesh):
    in_specs = (
        P("dp", "segment", None),
        P("segment", "dp", None, "mp"),
        P("segment", "mp", None),
        P("segment", None, None, "mp"),
        P("segment", "dp", None, "mp"),
        P("segment", "dp", None, "mp"),
        P("dp"),
        P("dp"),
    )
    out_specs = (P("segment", "mp", None), P("segment", None, None, "mp"), P("dp", "segment", None))
    sizes = (mesh.shape["segment"], mesh.shape["dp"], mesh.shape["mp"])
    return jax.shard_map(
        functools.partial(body, sizes=sizes),
        mesh=mesh, in_specs=in_specs, out_specs=out_specs, check_vma=False,
    )
```

```python
import functools

import jax
import jax.numpy as jnp
from jax import lax
from jax.experimental import pallas as pl
from jax.experimental.pallas import tpu as pltpu
from jax.sharding import PartitionSpec as P

HD = 128
TILES = 4
ADAPTER_SCALE = 2.0
F32 = jnp.float32
BF16 = jnp.bfloat16
NN = (((1,), (0,)), ((), ()))
NT = (((1,), (1,)), ((), ()))
TN = (((0,), (0,)), ((), ()))


def dot(a, b, dims):
    return lax.dot_general(a, b, dims, preferred_element_type=F32)


def flip(index, bit):
    return index + bit - 2 * bit * lax.rem(lax.div(index, bit), 2)


def bits_down(n):
    bits = []
    while n > 1:
        n //= 2
        bits.append(n)
    return bits


def kernel(
    sizes, parts,
    len_ref, tiles_ref, img_ref, up_ref, w_hbm, a_hbm, q_hbm, c_hbm,
    gdown_ref, gup_ref, gimg_ref,
    raw, w, a, q, c, xh, xq, low_p, low_r, low_b, kv_p, kv_r, dkv_own, dkv, back_p, back_r,
    g, zs, zr, fin, fr, load_sem, send_sem, recv_sem, *halves,
):
    S, D, M = sizes
    s, d, m = lax.axis_index("segment"), lax.axis_index("dp"), lax.axis_index("mp")
    rows_loc = xh.shape[1]
    nb = S * D
    rows = nb * rows_loc
    srows = S * rows_loc
    cw = w.shape[0]
    kvc = w.shape[1] // 2
    qw = a.shape[0]
    pw = cw // parts
    zw = pw // M
    s_bits, d_bits = bits_down(S), bits_down(D)

    def columns(at, size):
        return pl.ds(pl.multiple_of(at, 128), size)

    loads = [
        pltpu.make_async_copy(src, dst, load_sem.at[i])
        for i, (src, dst) in enumerate(
            [
                (img_ref.at[:, columns(d * cw, cw)], xh.at[d * S + s]),
                (img_ref.at[:, columns(m * qw, qw)], xq.at[d, s]),
                (a_hbm, a),
                (q_hbm, q),
                (c_hbm, c),
            ]
            + [(w_hbm.at[:, :, j * HD : (j + 1) * HD], raw.at[j]) for j in range(kvc // HD)]
        )
    ]
    for load in loads[5:] + loads[:5]:
        load.start()

    others = [(i, j) for i in range(D) for j in range(M) if i or j]
    barrier = pltpu.get_barrier_semaphore()
    peers = [(flip(s, b), d, m) for b in s_bits]
    peers += [(s, lax.rem(d + i, D), lax.rem(m + j, M)) for i, j in others]
    for peer in peers:
        pl.semaphore_signal(barrier, inc=1, device_id=peer, device_id_type=pl.DeviceIdType.MESH)
    pl.semaphore_wait(barrier, len(peers))

    started = []

    def send(src, dst, peer):
        k = len(started)
        copy = pltpu.make_async_remote_copy(
            src_ref=src, dst_ref=dst, send_sem=send_sem.at[k], recv_sem=recv_sem.at[k],
            device_id=peer, device_id_type=pl.DeviceIdType.MESH,
        )
        copy.start()
        started.append(copy)
        return copy

    steps = [("d", b) for b in d_bits] + [("s", b) for b in s_bits]

    def across(step, at):
        kind, b = step
        return (at[0], flip(at[1], b)) if kind == "d" else (flip(at[0], b), at[1])

    block = 128
    place = lax.broadcasted_iota(jnp.int32, (2 * block, 2 * block), 0)
    source = lax.broadcasted_iota(jnp.int32, (2 * block, 2 * block), 1)
    apart = jnp.where(
        source == jnp.where(place < block, 2 * place, 2 * (place - block) + 1), 1.0, 0.0
    ).astype(BF16)

    def separate(i, carry):
        at = pl.ds(pl.multiple_of(i * block, block), block)
        pairs = jnp.concatenate(
            [raw[j, at].reshape(2 * block, HD) for j in range(kvc // HD)], axis=1
        )
        sorted_rows = dot(apart, pairs, NN).astype(BF16)
        w[at, :kvc] = sorted_rows[:block]
        w[at, kvc:] = sorted_rows[block:]
        return carry

    me = (s, d)
    held = [[] for _ in steps]
    for k, step in enumerate(steps):
        to = across(step, me)
        half = img_ref.at[:, columns(to[1] * cw, cw)]
        held[k].append((send(half, xh.at[d * S + s], (*to, m)), "half", to))
        if step[0] == "s":
            quarter = img_ref.at[:, columns(m * qw, qw)]
            held[k].append((send(quarter, xq.at[d, s], (*to, m)), "quarter", to))
    for load in loads[5:]:
        load.wait()
    blocks = cw // block
    for k in range(len(steps)):
        lax.fori_loop(
            blocks * k // len(steps), blocks * (k + 1) // len(steps), separate, 0
        )
        for copy, kind, at in list(held[k]):
            copy.wait_recv()
            slot = xh.at[at[1] * S + at[0]] if kind == "half" else xq.at[d, at[0]]
            for later in range(k + 1, len(steps)):
                to = across(steps[later], me)
                held[later].append(
                    (send(slot, slot, (*to, m)), kind, across(steps[later], at))
                )

    ukk = jnp.concatenate([up_ref[0], jnp.zeros_like(up_ref[0])], axis=0)
    uvv = jnp.concatenate([jnp.zeros_like(up_ref[1]), up_ref[1]], axis=0)

    loads[0].wait()
    loads[1].wait()
    loads[2].wait()
    mine_q = xq[d].astype(F32).reshape(srows, qw).astype(BF16)
    low_p[...] = dot(mine_q, a[...], NN)
    low_c = [send(low_p, low_r.at[m], (s, d, lax.rem(m + j, M))) for j in range(1, M)]
    low_r[m] = low_p[...]

    xall = xh[...].astype(F32).reshape(rows, cw).astype(BF16)
    samples = [lax.rem(d + i, D) for i in range(1, D)]
    kv_c = []
    for n in range(2):
        kv_p[n] = dot(xall, w[:, n * kvc : (n + 1) * kvc], NN).reshape(D, srows, kvc)
        kv_c += [send(kv_p.at[n, to], kv_r.at[n, d], (s, to, m)) for to in samples]
        kv_r[n, d] = kv_p[n, d]
    xq_c = [send(xq.at[d], xq.at[d], (s, to, m)) for to in samples]
    for copy in low_c:
        copy.wait_recv()
    low_own = jnp.sum(low_r[...], axis=0).astype(BF16)
    low_b[d] = low_own
    lowb_c = [send(low_b.at[d], low_b.at[d], (s, to, m)) for to in samples]
    adapted = jnp.concatenate([dot(low_own, ukk, NN), dot(low_own, uvv, NN)], axis=1)
    for copy in kv_c:
        copy.wait_recv()
    frozen = jnp.concatenate([jnp.sum(kv_r[0], axis=0), jnp.sum(kv_r[1], axis=0)], axis=1)
    kv = (frozen + ADAPTER_SCALE * adapted).astype(BF16)

    loads[3].wait()
    loads[4].wait()
    text = q.shape[0]
    heads = q.shape[1] // HD
    kv_heads = kvc // HD
    group = heads // kv_heads
    cols = group * text
    live = (
        lax.rem(lax.broadcasted_iota(jnp.int32, (1, cols), 1), text) < len_ref[0]
    ).astype(F32)
    valid = lax.broadcasted_iota(jnp.int32, (srows, 1), 0) < tiles_ref[0] * (srows // TILES)
    for h in range(kv_heads):
        qs = jnp.concatenate(
            [q[:, (h * group + r) * HD : (h * group + r + 1) * HD] for r in range(group)], axis=0
        )
        cs = jnp.concatenate(
            [c[:, (h * group + r) * HD : (h * group + r + 1) * HD] for r in range(group)], axis=0
        )
        keys = kv[:, h * HD : (h + 1) * HD]
        vals = kv[:, kvc + h * HD : kvc + (h + 1) * HD]
        scores = jnp.where(valid, dot(keys, qs, NT) * HD ** (-0.5), -1e30)
        shifted = jnp.exp(scores - jnp.max(scores, axis=0, keepdims=True))
        att = shifted / jnp.sum(shifted, axis=0, keepdims=True)
        kept = (att.astype(BF16).astype(F32) * live).astype(BF16)
        dp = dot(vals, cs, NT)
        delta = jnp.sum(att * dp, axis=0, keepdims=True)
        ds = (att * (dp - delta) * live * HD ** (-0.5)).astype(BF16)
        dkv_own[:, h * HD : (h + 1) * HD] = dot(ds, qs, NN).astype(BF16)
        dkv_own[:, kvc + h * HD : kvc + (h + 1) * HD] = dot(kept, cs, NN).astype(BF16)

    dkv_c = [send(dkv_own, dkv.at[d], (s, to, m)) for to in samples]
    own = dkv_own[...]
    dkv[d] = own
    back_p[...] = ADAPTER_SCALE * (dot(own[:, :kvc], ukk, NT) + dot(own[:, kvc:], uvv, NT))
    back_c = [
        send(back_p, back_r.at[d, m], (s, lax.rem(d + i, D), lax.rem(m + j, M)))
        for i, j in others
    ]
    back_r[d, m] = back_p[...]
    for copy in dkv_c:
        copy.wait_recv()
    dall = dkv[...].reshape(rows, 2 * kvc)

    step = min(cw, 1024)
    for j in range(0, cw, step):
        g[:, :, j : j + step] = dot(dall, w[j : j + step, :], NT).reshape(nb, rows_loc, step)

    for copy in back_c:
        copy.wait_recv()
    back = jnp.sum(back_r[...], axis=1).reshape(rows, back_r.shape[3]).astype(BF16)

    if cw >= qw:
        @pl.when(lax.div(m, cw // qw) == d)
        def _():
            at = columns(lax.rem(m, cw // qw) * qw, qw)
            g[:, :, at] = g[:, :, at] + dot(back, a[...], NT).reshape(nb, rows_loc, qw)
    else:
        @pl.when(lax.div(d, qw // cw) == m)
        def _():
            at = columns(lax.rem(d, qw // cw) * cw, cw)
            g[...] = g[...] + dot(back, a[at, :], NT).reshape(nb, rows_loc, cw)

    def adapter_up():
        for copy in lowb_c:
            copy.wait_recv()
        low = low_b[...].reshape(rows, low_b.shape[2])
        rank = low.shape[1] // 2
        gup_ref[0] = (ADAPTER_SCALE * dot(low, dall[:, :kvc], TN)[:rank]).astype(BF16)
        gup_ref[1] = (ADAPTER_SCALE * dot(low, dall[:, kvc:], TN)[rank:]).astype(BF16)

    def adapter_down():
        for copy in xq_c:
            copy.wait_recv()
        all_q = xq[...].astype(F32).reshape(rows, qw).astype(BF16)
        gdown_ref[...] = dot(all_q, back, TN).astype(BF16)

    ladder = list(reversed(s_bits))
    flying = {}

    def halve_send(n, p):
        b = ladder[n]
        count = S // (2 * b)
        theirs = lax.rem(s, b) + b * (1 - lax.rem(lax.div(s, b), 2))
        for i in range(D):
            for t in range(count):
                halves[2 * n][p, i * count + t] = g[
                    i * S + theirs + 2 * b * t, :, p * pw : (p + 1) * pw
                ].astype(BF16)
        flying[p] = [send(halves[2 * n].at[p], halves[2 * n + 1].at[p], (flip(s, b), d, m))]

    def halve_take(n, p):
        b = ladder[n]
        count = S // (2 * b)
        ours = lax.rem(s, b) + b * lax.rem(lax.div(s, b), 2)
        flying[p][0].wait_recv()
        for i in range(D):
            for t in range(count):
                at = i * S + ours + 2 * b * t
                g[at, :, p * pw : (p + 1) * pw] = g[at, :, p * pw : (p + 1) * pw] + halves[
                    2 * n + 1
                ][p, i * count + t].astype(F32)

    def group_send(p):
        for j in range(1, M):
            to = lax.rem(m + j, M)
            for i in range(D):
                zs[p, j - 1, i] = g[i * S + s, :, columns(p * pw + to * zw, zw)].astype(BF16)
        flying[p] = [
            send(zs.at[p, j - 1], zr.at[p, j - 1], (s, d, lax.rem(m + j, M)))
            for j in range(1, M)
        ]

    def group_take(p):
        for copy in flying[p]:
            copy.wait_recv()
        for i in range(D):
            total = g[i * S + s, :, columns(p * pw + m * zw, zw)]
            for j in range(M - 1):
                total = total + zr[p, j, i].astype(F32)
            fin[p, i] = total.astype(BF16)
        flying[p] = []
        for i, j in others:
            to = lax.rem(d + i, D)
            flying[p].append(
                send(fin.at[p, to], fr.at[p, d * M + m], (s, to, lax.rem(m + j, M)))
            )
        fr[p, d * M + m] = fin[p, d]

    def finish(p):
        for copy in flying[p]:
            copy.wait_recv()
        for i in range(D):
            for j in range(M):
                at = i * cw + p * pw + j * zw
                gimg_ref[:, at : at + zw] = fr[p, i * M + j].astype(F32)

    for p in range(parts):
        halve_send(0, p)
    adapter_up()
    stages = []
    for n in range(1, len(ladder)):
        stages.append(lambda p, n=n: (halve_take(n - 1, p), halve_send(n, p)))
    stages.append(lambda p: (halve_take(len(ladder) - 1, p), group_send(p)))
    stages.append(group_take)
    stages.append(finish)
    for t in range(parts + len(stages) - 1):
        for k, stage in enumerate(stages):
            if 0 <= t - k < parts:
                stage(t - k)
        if t == parts - 1:
            adapter_down()
    for copy in started:
        copy.wait_send()


def deliver(x0, x1, x2, y0, y1, y2, sems):
    copies = [
        pltpu.make_async_copy(x, y, sems.at[i])
        for i, (x, y) in enumerate([(x0, y0), (x1, y1), (x2, y2)])
    ]
    for copy in copies:
        copy.start()
    for copy in copies:
        copy.wait()


def body(
    encoder_image_states,
    frozen_key_value,
    adapter_down_weight,
    adapter_up_weight,
    queries,
    cotangent,
    text_token_length,
    image_tile_count,
    *,
    sizes,
):
    S, D, M = sizes
    rows_loc, width = encoder_image_states.shape[1:]
    cw, kvc = frozen_key_value.shape[1], frozen_key_value.shape[3]
    qw, ranks = adapter_down_weight.shape[1:]
    text, qcols = queries.shape[2:]
    nb = S * D
    rows, srows = nb * rows_loc, S * rows_loc
    parts = max(1, min(2, cw // M // 128))
    pw = cw // parts
    zw = pw // M
    vmem = pl.BlockSpec(memory_space=pltpu.VMEM)
    smem = pl.BlockSpec(memory_space=pltpu.SMEM)
    hbm = pl.BlockSpec(memory_space=pl.ANY)
    halves = []
    bits = bits_down(S)
    for b in reversed(bits):
        halves += [pltpu.VMEM((parts, D * S // (2 * b), rows_loc, pw), BF16)] * 2
    sends = (nb - 1) + (S - 1) + (M - 1) + 5 * (D - 1) + (D * M - 1)
    sends += parts * (len(bits) + (M - 1) + (D * M - 1))
    shapes = (
        jax.ShapeDtypeStruct((qw, ranks), BF16),
        jax.ShapeDtypeStruct(adapter_up_weight.shape[1:], BF16),
        jax.ShapeDtypeStruct((rows_loc, width), F32),
    )
    down, up, image = pl.pallas_call(
        functools.partial(kernel, sizes, parts),
        out_shape=shapes,
        in_specs=[smem, smem, hbm, vmem, hbm, hbm, hbm, hbm],
        out_specs=(vmem, vmem, vmem),
        scratch_shapes=[
            pltpu.VMEM((kvc // HD, cw, 2, HD), BF16),
            pltpu.VMEM((cw, 2 * kvc), BF16),
            pltpu.VMEM((qw, ranks), BF16),
            pltpu.VMEM((text, qcols), BF16),
            pltpu.VMEM((text, qcols), BF16),
            pltpu.VMEM((nb, rows_loc, cw), BF16),
            pltpu.VMEM((D, S, rows_loc, qw), BF16),
            pltpu.VMEM((srows, ranks), F32),
            pltpu.VMEM((M, srows, ranks), F32),
            pltpu.VMEM((D, srows, ranks), BF16),
            pltpu.VMEM((2, D, srows, kvc), F32),
            pltpu.VMEM((2, D, srows, kvc), F32),
            pltpu.VMEM((srows, 2 * kvc), BF16),
            pltpu.VMEM((D, srows, 2 * kvc), BF16),
            pltpu.VMEM((srows, ranks), F32),
            pltpu.VMEM((D, M, srows, ranks), F32),
            pltpu.VMEM((nb, rows_loc, cw), F32),
            pltpu.VMEM((parts, M - 1, D, rows_loc, zw), BF16),
            pltpu.VMEM((parts, M - 1, D, rows_loc, zw), BF16),
            pltpu.VMEM((parts, D, rows_loc, zw), BF16),
            pltpu.VMEM((parts, D * M, rows_loc, zw), BF16),
            pltpu.SemaphoreType.DMA((5 + kvc // HD,)),
            pltpu.SemaphoreType.DMA((sends,)),
            pltpu.SemaphoreType.DMA((sends,)),
            *halves,
        ],
        compiler_params=pltpu.CompilerParams(
            collective_id=0, has_side_effects=True, vmem_limit_bytes=58 * 2**20
        ),
    )(
        text_token_length,
        image_tile_count,
        encoder_image_states[0],
        adapter_up_weight[0],
        frozen_key_value[0],
        adapter_down_weight[0],
        queries[0, 0],
        cotangent[0, 0],
    )
    down, up, image = pl.pallas_call(
        deliver,
        out_shape=shapes,
        in_specs=[vmem] * 3,
        out_specs=(hbm,) * 3,
        scratch_shapes=[pltpu.SemaphoreType.DMA((3,))],
    )(down, up, image)
    return down[None], up[None], image[None]


def solution(mesh):
    in_specs = (
        P("dp", "segment", None),
        P("segment", "dp", None, "mp"),
        P("segment", "mp", None),
        P("segment", None, None, "mp"),
        P("segment", "dp", None, "mp"),
        P("segment", "dp", None, "mp"),
        P("dp"),
        P("dp"),
    )
    out_specs = (P("segment", "mp", None), P("segment", None, None, "mp"), P("dp", "segment", None))
    sizes = (mesh.shape["segment"], mesh.shape["dp"], mesh.shape["mp"])
    return jax.shard_map(
        functools.partial(body, sizes=sizes),
        mesh=mesh, in_specs=in_specs, out_specs=out_specs, check_vma=False,
    )
```

```python
import functools

import jax
import jax.numpy as jnp
from jax import lax
from jax.experimental import pallas as pl
from jax.experimental.pallas import tpu as pltpu
from jax.sharding import PartitionSpec as P

HD = 128
TILES = 4
ADAPTER_SCALE = 2.0
F32 = jnp.float32
BF16 = jnp.bfloat16
NN = (((1,), (0,)), ((), ()))
NT = (((1,), (1,)), ((), ()))
TN = (((0,), (0,)), ((), ()))


def dot(a, b, dims):
    return lax.dot_general(a, b, dims, preferred_element_type=F32)


def flip(index, bit):
    return index + bit - 2 * bit * lax.rem(lax.div(index, bit), 2)


def bits_down(n):
    bits = []
    while n > 1:
        n //= 2
        bits.append(n)
    return bits


def kernel(
    sizes, parts,
    len_ref, tiles_ref, img_ref, up_hbm, w_hbm, a_hbm, q_hbm, c_hbm,
    gdown_hbm, gup_hbm, gimg_hbm,
    up_ref, gdown_ref, gup_ref, raw, w, a, q, c, xh, xq, low_p, low_r, low_b, kv_p, kv_r, dkv_own, dkv, back_p, back_r,
    g, zs, zr, fin, fr, load_sem, store_sem, send_sem, recv_sem, *halves,
):
    S, D, M = sizes
    s, d, m = lax.axis_index("segment"), lax.axis_index("dp"), lax.axis_index("mp")
    rows_loc = xh.shape[1]
    nb = S * D
    rows = nb * rows_loc
    srows = S * rows_loc
    cw = w.shape[0]
    kvc = w.shape[1] // 2
    qw = a.shape[0]
    pw = cw // parts
    zw = pw // M
    s_bits, d_bits = bits_down(S), bits_down(D)

    def columns(at, size):
        return pl.ds(pl.multiple_of(at, 128), size)

    loads = [
        pltpu.make_async_copy(src, dst, load_sem.at[i])
        for i, (src, dst) in enumerate(
            [
                (img_ref.at[:, columns(d * cw, cw)], xh.at[d * S + s]),
                (img_ref.at[:, columns(m * qw, qw)], xq.at[d, s]),
                (a_hbm, a),
                (q_hbm, q),
                (c_hbm, c),
                (up_hbm, up_ref),
            ]
            + [(w_hbm.at[:, :, j * HD : (j + 1) * HD], raw.at[j]) for j in range(kvc // HD)]
        )
    ]
    for load in loads[6:] + loads[:6]:
        load.start()

    others = [(i, j) for i in range(D) for j in range(M) if i or j]
    barrier = pltpu.get_barrier_semaphore()
    peers = [(flip(s, b), d, m) for b in s_bits]
    peers += [(s, lax.rem(d + i, D), lax.rem(m + j, M)) for i, j in others]
    for peer in peers:
        pl.semaphore_signal(barrier, inc=1, device_id=peer, device_id_type=pl.DeviceIdType.MESH)
    pl.semaphore_wait(barrier, len(peers))

    started = []

    def send(src, dst, peer):
        k = len(started)
        copy = pltpu.make_async_remote_copy(
            src_ref=src, dst_ref=dst, send_sem=send_sem.at[k], recv_sem=recv_sem.at[k],
            device_id=peer, device_id_type=pl.DeviceIdType.MESH,
        )
        copy.start()
        started.append(copy)
        return copy

    steps = [("d", b) for b in d_bits] + [("s", b) for b in s_bits]

    def across(step, at):
        kind, b = step
        return (at[0], flip(at[1], b)) if kind == "d" else (flip(at[0], b), at[1])

    block = 128
    place = lax.broadcasted_iota(jnp.int32, (2 * block, 2 * block), 0)
    source = lax.broadcasted_iota(jnp.int32, (2 * block, 2 * block), 1)
    apart = jnp.where(
        source == jnp.where(place < block, 2 * place, 2 * (place - block) + 1), 1.0, 0.0
    ).astype(BF16)

    def separate(i, carry):
        at = pl.ds(pl.multiple_of(i * block, block), block)
        pairs = jnp.concatenate(
            [raw[j, at].reshape(2 * block, HD) for j in range(kvc // HD)], axis=1
        )
        sorted_rows = dot(apart, pairs, NN).astype(BF16)
        w[at, :kvc] = sorted_rows[:block]
        w[at, kvc:] = sorted_rows[block:]
        return carry

    me = (s, d)
    held = [[] for _ in steps]
    for k, step in enumerate(steps):
        to = across(step, me)
        half = img_ref.at[:, columns(to[1] * cw, cw)]
        held[k].append((send(half, xh.at[d * S + s], (*to, m)), "half", to))
        if step[0] == "s":
            quarter = img_ref.at[:, columns(m * qw, qw)]
            held[k].append((send(quarter, xq.at[d, s], (*to, m)), "quarter", to))
    for load in loads[6:]:
        load.wait()
    blocks = cw // block
    for k in range(len(steps)):
        lax.fori_loop(
            blocks * k // len(steps), blocks * (k + 1) // len(steps), separate, 0
        )
        for copy, kind, at in list(held[k]):
            copy.wait_recv()
            slot = xh.at[at[1] * S + at[0]] if kind == "half" else xq.at[d, at[0]]
            for later in range(k + 1, len(steps)):
                to = across(steps[later], me)
                held[later].append(
                    (send(slot, slot, (*to, m)), kind, across(steps[later], at))
                )

    loads[5].wait()
    ukk = jnp.concatenate([up_ref[0], jnp.zeros_like(up_ref[0])], axis=0)
    uvv = jnp.concatenate([jnp.zeros_like(up_ref[1]), up_ref[1]], axis=0)

    loads[0].wait()
    loads[1].wait()
    loads[2].wait()
    mine_q = xq[d].astype(F32).reshape(srows, qw).astype(BF16)
    low_p[...] = dot(mine_q, a[...], NN)
    low_c = [send(low_p, low_r.at[m], (s, d, lax.rem(m + j, M))) for j in range(1, M)]
    low_r[m] = low_p[...]

    xall = xh[...].astype(F32).reshape(rows, cw).astype(BF16)
    samples = [lax.rem(d + i, D) for i in range(1, D)]
    kv_c = []
    for n in range(2):
        kv_p[n] = dot(xall, w[:, n * kvc : (n + 1) * kvc], NN).reshape(D, srows, kvc)
        kv_c += [send(kv_p.at[n, to], kv_r.at[n, d], (s, to, m)) for to in samples]
        kv_r[n, d] = kv_p[n, d]
    xq_c = [send(xq.at[d], xq.at[d], (s, to, m)) for to in samples]
    for copy in low_c:
        copy.wait_recv()
    low_own = jnp.sum(low_r[...], axis=0).astype(BF16)
    low_b[d] = low_own
    lowb_c = [send(low_b.at[d], low_b.at[d], (s, to, m)) for to in samples]
    adapted = jnp.concatenate([dot(low_own, ukk, NN), dot(low_own, uvv, NN)], axis=1)
    for copy in kv_c:
        copy.wait_recv()
    frozen = jnp.concatenate([jnp.sum(kv_r[0], axis=0), jnp.sum(kv_r[1], axis=0)], axis=1)
    kv = (frozen + ADAPTER_SCALE * adapted).astype(BF16)

    loads[3].wait()
    loads[4].wait()
    text = q.shape[0]
    heads = q.shape[1] // HD
    kv_heads = kvc // HD
    group = heads // kv_heads
    cols = group * text
    live = (
        lax.rem(lax.broadcasted_iota(jnp.int32, (1, cols), 1), text) < len_ref[0]
    ).astype(F32)
    valid = lax.broadcasted_iota(jnp.int32, (srows, 1), 0) < tiles_ref[0] * (srows // TILES)
    for h in range(kv_heads):
        qs = jnp.concatenate(
            [q[:, (h * group + r) * HD : (h * group + r + 1) * HD] for r in range(group)], axis=0
        )
        cs = jnp.concatenate(
            [c[:, (h * group + r) * HD : (h * group + r + 1) * HD] for r in range(group)], axis=0
        )
        keys = kv[:, h * HD : (h + 1) * HD]
        vals = kv[:, kvc + h * HD : kvc + (h + 1) * HD]
        scores = jnp.where(valid, dot(keys, qs, NT) * HD ** (-0.5), -1e30)
        shifted = jnp.exp(scores - jnp.max(scores, axis=0, keepdims=True))
        att = shifted / jnp.sum(shifted, axis=0, keepdims=True)
        kept = (att.astype(BF16).astype(F32) * live).astype(BF16)
        dp = dot(vals, cs, NT)
        delta = jnp.sum(att * dp, axis=0, keepdims=True)
        ds = (att * (dp - delta) * live * HD ** (-0.5)).astype(BF16)
        dkv_own[:, h * HD : (h + 1) * HD] = dot(ds, qs, NN).astype(BF16)
        dkv_own[:, kvc + h * HD : kvc + (h + 1) * HD] = dot(kept, cs, NN).astype(BF16)

    dkv_c = [send(dkv_own, dkv.at[d], (s, to, m)) for to in samples]
    own = dkv_own[...]
    dkv[d] = own
    back_p[...] = ADAPTER_SCALE * (dot(own[:, :kvc], ukk, NT) + dot(own[:, kvc:], uvv, NT))
    back_c = [
        send(back_p, back_r.at[d, m], (s, lax.rem(d + i, D), lax.rem(m + j, M)))
        for i, j in others
    ]
    back_r[d, m] = back_p[...]
    for copy in dkv_c:
        copy.wait_recv()
    dall = dkv[...].reshape(rows, 2 * kvc)

    step = min(cw, 1024)
    for j in range(0, cw, step):
        g[:, :, j : j + step] = dot(dall, w[j : j + step, :], NT).reshape(nb, rows_loc, step)

    for copy in back_c:
        copy.wait_recv()
    back = jnp.sum(back_r[...], axis=1).reshape(rows, back_r.shape[3]).astype(BF16)

    if cw >= qw:
        @pl.when(lax.div(m, cw // qw) == d)
        def _():
            at = columns(lax.rem(m, cw // qw) * qw, qw)
            g[:, :, at] = g[:, :, at] + dot(back, a[...], NT).reshape(nb, rows_loc, qw)
    else:
        @pl.when(lax.div(d, qw // cw) == m)
        def _():
            at = columns(lax.rem(d, qw // cw) * cw, cw)
            g[...] = g[...] + dot(back, a[at, :], NT).reshape(nb, rows_loc, cw)

    def adapter_up():
        for copy in lowb_c:
            copy.wait_recv()
        low = low_b[...].reshape(rows, low_b.shape[2])
        rank = low.shape[1] // 2
        gup_ref[0] = (ADAPTER_SCALE * dot(low, dall[:, :kvc], TN)[:rank]).astype(BF16)
        gup_ref[1] = (ADAPTER_SCALE * dot(low, dall[:, kvc:], TN)[rank:]).astype(BF16)
        store(gup_ref, gup_hbm)

    def adapter_down():
        for copy in xq_c:
            copy.wait_recv()
        all_q = xq[...].astype(F32).reshape(rows, qw).astype(BF16)
        gdown_ref[...] = dot(all_q, back, TN).astype(BF16)
        store(gdown_ref, gdown_hbm)

    ladder = list(reversed(s_bits))
    flying = {}

    def halve_send(n, p):
        b = ladder[n]
        count = S // (2 * b)
        theirs = lax.rem(s, b) + b * (1 - lax.rem(lax.div(s, b), 2))
        for i in range(D):
            for t in range(count):
                halves[2 * n][p, i * count + t] = g[
                    i * S + theirs + 2 * b * t, :, p * pw : (p + 1) * pw
                ].astype(BF16)
        flying[p] = [send(halves[2 * n].at[p], halves[2 * n + 1].at[p], (flip(s, b), d, m))]

    def halve_take(n, p):
        b = ladder[n]
        count = S // (2 * b)
        ours = lax.rem(s, b) + b * lax.rem(lax.div(s, b), 2)
        flying[p][0].wait_recv()
        for i in range(D):
            for t in range(count):
                at = i * S + ours + 2 * b * t
                g[at, :, p * pw : (p + 1) * pw] = g[at, :, p * pw : (p + 1) * pw] + halves[
                    2 * n + 1
                ][p, i * count + t].astype(F32)

    def group_send(p):
        for j in range(1, M):
            to = lax.rem(m + j, M)
            for i in range(D):
                zs[p, j - 1, i] = g[i * S + s, :, columns(p * pw + to * zw, zw)].astype(BF16)
        flying[p] = [
            send(zs.at[p, j - 1], zr.at[p, j - 1], (s, d, lax.rem(m + j, M)))
            for j in range(1, M)
        ]

    def group_take(p):
        for copy in flying[p]:
            copy.wait_recv()
        for i in range(D):
            total = g[i * S + s, :, columns(p * pw + m * zw, zw)]
            for j in range(M - 1):
                total = total + zr[p, j, i].astype(F32)
            fin[p, i] = total.astype(BF16)
        flying[p] = []
        for i, j in others:
            to = lax.rem(d + i, D)
            flying[p].append(
                send(fin.at[p, to], fr.at[p, d * M + m], (s, to, lax.rem(m + j, M)))
            )
        fr[p, d * M + m] = fin[p, d]

    stores = []

    def store(src, dst):
        copy = pltpu.make_async_copy(src, dst, store_sem.at[len(stores)])
        copy.start()
        stores.append(copy)

    def finish(p):
        for copy in flying[p]:
            copy.wait_recv()
        store(fr.at[p], gimg_hbm.at[p])

    for p in range(parts):
        halve_send(0, p)
    stages = []
    for n in range(1, len(ladder)):
        stages.append(lambda p, n=n: (halve_take(n - 1, p), halve_send(n, p)))
    stages.append(lambda p: (halve_take(len(ladder) - 1, p), group_send(p)))
    stages.append(group_take)
    stages.append(finish)
    for t in range(parts + len(stages) - 1):
        for k, stage in enumerate(stages):
            if k == len(stages) - 1 and t == parts + k - 2:
                adapter_down()
            if 0 <= t - k < parts:
                stage(t - k)
            if k == 0 and t == min(1, parts - 1):
                adapter_up()
    for copy in stores:
        copy.wait()
    for copy in started:
        copy.wait_send()


def deliver(sizes, parts, x0, x1, x2, y0, y1, y2, wide, sems):
    D, M = sizes
    zw = x2.shape[3]
    copies = [
        pltpu.make_async_copy(x, y, sems.at[i])
        for i, (x, y) in enumerate([(x0, y0), (x1, y1), (wide, y2)])
    ]
    copies[0].start()
    copies[1].start()
    for i in range(D):
        for p in range(parts):
            for j in range(M):
                at = ((i * parts + p) * M + j) * zw
                wide[:, at : at + zw] = x2[p, i * M + j].astype(F32)
    copies[2].start()
    for copy in copies:
        copy.wait()


def body(
    encoder_image_states,
    frozen_key_value,
    adapter_down_weight,
    adapter_up_weight,
    queries,
    cotangent,
    text_token_length,
    image_tile_count,
    *,
    sizes,
):
    S, D, M = sizes
    rows_loc, width = encoder_image_states.shape[1:]
    cw, kvc = frozen_key_value.shape[1], frozen_key_value.shape[3]
    qw, ranks = adapter_down_weight.shape[1:]
    text, qcols = queries.shape[2:]
    nb = S * D
    rows, srows = nb * rows_loc, S * rows_loc
    parts = max(1, min(4, cw // M // 128))
    pw = cw // parts
    zw = pw // M
    vmem = pl.BlockSpec(memory_space=pltpu.VMEM)
    smem = pl.BlockSpec(memory_space=pltpu.SMEM)
    hbm = pl.BlockSpec(memory_space=pl.ANY)
    halves = []
    bits = bits_down(S)
    for b in reversed(bits):
        halves += [pltpu.VMEM((parts, D * S // (2 * b), rows_loc, pw), BF16)] * 2
    sends = (nb - 1) + (S - 1) + (M - 1) + 5 * (D - 1) + (D * M - 1)
    sends += parts * (len(bits) + (M - 1) + (D * M - 1))
    shapes = (
        jax.ShapeDtypeStruct((qw, ranks), BF16),
        jax.ShapeDtypeStruct(adapter_up_weight.shape[1:], BF16),
        jax.ShapeDtypeStruct((rows_loc, width), F32),
    )
    down, up, image = pl.pallas_call(
        functools.partial(kernel, sizes, parts),
        out_shape=(*shapes[:2], jax.ShapeDtypeStruct((parts, D * M, rows_loc, zw), BF16)),
        in_specs=[smem, smem] + [hbm] * 6,
        out_specs=(hbm, hbm, hbm),
        scratch_shapes=[
            pltpu.VMEM(adapter_up_weight.shape[1:], BF16),
            pltpu.VMEM((qw, ranks), BF16),
            pltpu.VMEM(adapter_up_weight.shape[1:], BF16),
            pltpu.VMEM((kvc // HD, cw, 2, HD), BF16),
            pltpu.VMEM((cw, 2 * kvc), BF16),
            pltpu.VMEM((qw, ranks), BF16),
            pltpu.VMEM((text, qcols), BF16),
            pltpu.VMEM((text, qcols), BF16),
            pltpu.VMEM((nb, rows_loc, cw), BF16),
            pltpu.VMEM((D, S, rows_loc, qw), BF16),
            pltpu.VMEM((srows, ranks), F32),
            pltpu.VMEM((M, srows, ranks), F32),
            pltpu.VMEM((D, srows, ranks), BF16),
            pltpu.VMEM((2, D, srows, kvc), F32),
            pltpu.VMEM((2, D, srows, kvc), F32),
            pltpu.VMEM((srows, 2 * kvc), BF16),
            pltpu.VMEM((D, srows, 2 * kvc), BF16),
            pltpu.VMEM((srows, ranks), F32),
            pltpu.VMEM((D, M, srows, ranks), F32),
            pltpu.VMEM((nb, rows_loc, cw), F32),
            pltpu.VMEM((parts, M - 1, D, rows_loc, zw), BF16),
            pltpu.VMEM((parts, M - 1, D, rows_loc, zw), BF16),
            pltpu.VMEM((parts, D, rows_loc, zw), BF16),
            pltpu.VMEM((parts, D * M, rows_loc, zw), BF16),
            pltpu.SemaphoreType.DMA((6 + kvc // HD,)),
            pltpu.SemaphoreType.DMA((2 + parts,)),
            pltpu.SemaphoreType.DMA((sends,)),
            pltpu.SemaphoreType.DMA((sends,)),
            *halves,
        ],
        compiler_params=pltpu.CompilerParams(
            collective_id=0, has_side_effects=True, vmem_limit_bytes=58 * 2**20
        ),
    )(
        text_token_length,
        image_tile_count,
        encoder_image_states[0],
        adapter_up_weight[0],
        frozen_key_value[0],
        adapter_down_weight[0],
        queries[0, 0],
        cotangent[0, 0],
    )
    down, up, image = pl.pallas_call(
        functools.partial(deliver, (D, M), parts),
        out_shape=shapes,
        in_specs=[vmem] * 3,
        out_specs=(hbm,) * 3,
        scratch_shapes=[pltpu.VMEM((rows_loc, width), F32), pltpu.SemaphoreType.DMA((3,))],
    )(down, up, image)
    return down[None], up[None], image[None]


def solution(mesh):
    in_specs = (
        P("dp", "segment", None),
        P("segment", "dp", None, "mp"),
        P("segment", "mp", None),
        P("segment", None, None, "mp"),
        P("segment", "dp", None, "mp"),
        P("segment", "dp", None, "mp"),
        P("dp"),
        P("dp"),
    )
    out_specs = (P("segment", "mp", None), P("segment", None, None, "mp"), P("dp", "segment", None))
    sizes = (mesh.shape["segment"], mesh.shape["dp"], mesh.shape["mp"])
    return jax.shard_map(
        functools.partial(body, sizes=sizes),
        mesh=mesh, in_specs=in_specs, out_specs=out_specs, check_vma=False,
    )
```

```python
import functools

import jax
import jax.numpy as jnp
from jax import lax
from jax.experimental import pallas as pl
from jax.experimental.pallas import tpu as pltpu
from jax.sharding import PartitionSpec as P

HD = 128
TILES = 4
ADAPTER_SCALE = 2.0
F32 = jnp.float32
BF16 = jnp.bfloat16
NN = (((1,), (0,)), ((), ()))
NT = (((1,), (1,)), ((), ()))
TN = (((0,), (0,)), ((), ()))


def dot(a, b, dims):
    return lax.dot_general(a, b, dims, preferred_element_type=F32)


def flip(index, bit):
    return index + bit - 2 * bit * lax.rem(lax.div(index, bit), 2)


def bits_down(n):
    bits = []
    while n > 1:
        n //= 2
        bits.append(n)
    return bits


def kernel(
    sizes, parts,
    len_ref, tiles_ref, img_ref, up_hbm, w_hbm, a_hbm, q_hbm, c_hbm,
    gdown_hbm, gup_hbm, gimg_hbm,
    up_ref, gdown_ref, gup_ref, raw, w, a, q, c, xh, xq, low_p, low_r, low_b, kv_p, kv_r, dkv_own, dkv, back_p, back_r,
    g, zs, zr, fin, fr, load_sem, store_sem, send_sem, recv_sem, *halves,
):
    S, D, M = sizes
    s, d, m = lax.axis_index("segment"), lax.axis_index("dp"), lax.axis_index("mp")
    rows_loc = xh.shape[1]
    nb = S * D
    rows = nb * rows_loc
    srows = S * rows_loc
    cw = w.shape[0]
    kvc = w.shape[1] // 2
    qw = a.shape[0]
    pw = cw // parts
    zw = pw // M
    s_bits, d_bits = bits_down(S), bits_down(D)

    def columns(at, size):
        return pl.ds(pl.multiple_of(at, 128), size)

    loads = [
        pltpu.make_async_copy(src, dst, load_sem.at[i])
        for i, (src, dst) in enumerate(
            [
                (img_ref.at[:, columns(d * cw, cw)], xh.at[d * S + s]),
                (img_ref.at[:, columns(m * qw, qw)], xq.at[d, s]),
                (a_hbm, a),
                (q_hbm, q),
                (c_hbm, c),
                (up_hbm, up_ref),
            ]
            + [(w_hbm.at[:, :, j * HD : (j + 1) * HD], raw.at[j]) for j in range(kvc // HD)]
        )
    ]
    for load in loads[6:] + loads[:6]:
        load.start()

    others = [(i, j) for i in range(D) for j in range(M) if i or j]
    barrier = pltpu.get_barrier_semaphore()
    peers = [(flip(s, b), d, m) for b in s_bits]
    peers += [(s, lax.rem(d + i, D), lax.rem(m + j, M)) for i, j in others]
    for peer in peers:
        pl.semaphore_signal(barrier, inc=1, device_id=peer, device_id_type=pl.DeviceIdType.MESH)
    pl.semaphore_wait(barrier, len(peers))

    started = []

    def send(src, dst, peer):
        k = len(started)
        copy = pltpu.make_async_remote_copy(
            src_ref=src, dst_ref=dst, send_sem=send_sem.at[k], recv_sem=recv_sem.at[k],
            device_id=peer, device_id_type=pl.DeviceIdType.MESH,
        )
        copy.start()
        started.append(copy)
        return copy

    steps = [("d", b) for b in d_bits] + [("s", b) for b in s_bits]

    def across(step, at):
        kind, b = step
        return (at[0], flip(at[1], b)) if kind == "d" else (flip(at[0], b), at[1])

    block = 128
    place = lax.broadcasted_iota(jnp.int32, (2 * block, 2 * block), 0)
    source = lax.broadcasted_iota(jnp.int32, (2 * block, 2 * block), 1)
    apart = jnp.where(
        source == jnp.where(place < block, 2 * place, 2 * (place - block) + 1), 1.0, 0.0
    ).astype(BF16)

    def separate(i, carry):
        at = pl.ds(pl.multiple_of(i * block, block), block)
        pairs = jnp.concatenate(
            [raw[j, at].reshape(2 * block, HD) for j in range(kvc // HD)], axis=1
        )
        sorted_rows = dot(apart, pairs, NN).astype(BF16)
        w[at, :kvc] = sorted_rows[:block]
        w[at, kvc:] = sorted_rows[block:]
        return carry

    me = (s, d)
    held = [[] for _ in steps]
    for k, step in enumerate(steps):
        to = across(step, me)
        half = img_ref.at[:, columns(to[1] * cw, cw)]
        held[k].append((send(half, xh.at[d * S + s], (*to, m)), "half", to))
        if step[0] == "s":
            quarter = img_ref.at[:, columns(m * qw, qw)]
            held[k].append((send(quarter, xq.at[d, s], (*to, m)), "quarter", to))
    for load in loads[6:]:
        load.wait()
    blocks = cw // block
    for k in range(len(steps)):
        lax.fori_loop(
            blocks * k // len(steps), blocks * (k + 1) // len(steps), separate, 0
        )
        for copy, kind, at in list(held[k]):
            copy.wait_recv()
            slot = xh.at[at[1] * S + at[0]] if kind == "half" else xq.at[d, at[0]]
            for later in range(k + 1, len(steps)):
                to = across(steps[later], me)
                held[later].append(
                    (send(slot, slot, (*to, m)), kind, across(steps[later], at))
                )

    loads[5].wait()
    ukk = jnp.concatenate([up_ref[0], jnp.zeros_like(up_ref[0])], axis=0)
    uvv = jnp.concatenate([jnp.zeros_like(up_ref[1]), up_ref[1]], axis=0)

    loads[0].wait()
    loads[1].wait()
    loads[2].wait()
    mine_q = xq[d].astype(F32).reshape(srows, qw).astype(BF16)
    low_p[...] = dot(mine_q, a[...], NN)
    low_c = [send(low_p, low_r.at[m], (s, d, lax.rem(m + j, M))) for j in range(1, M)]
    low_r[m] = low_p[...]

    xall = xh[...].astype(F32).reshape(rows, cw).astype(BF16)
    samples = [lax.rem(d + i, D) for i in range(1, D)]
    kv_c = []
    for n in range(2):
        kv_p[n] = dot(xall, w[:, n * kvc : (n + 1) * kvc], NN).reshape(D, srows, kvc)
        kv_c += [send(kv_p.at[n, to], kv_r.at[n, d], (s, to, m)) for to in samples]
        kv_r[n, d] = kv_p[n, d]
    xq_c = [send(xq.at[d], xq.at[d], (s, to, m)) for to in samples]
    for copy in low_c:
        copy.wait_recv()
    low_own = jnp.sum(low_r[...], axis=0).astype(BF16)
    low_b[d] = low_own
    lowb_c = [send(low_b.at[d], low_b.at[d], (s, to, m)) for to in samples]
    adapted = jnp.concatenate([dot(low_own, ukk, NN), dot(low_own, uvv, NN)], axis=1)
    for copy in kv_c:
        copy.wait_recv()
    frozen = jnp.concatenate([jnp.sum(kv_r[0], axis=0), jnp.sum(kv_r[1], axis=0)], axis=1)
    kv = (frozen + ADAPTER_SCALE * adapted).astype(BF16)

    loads[3].wait()
    loads[4].wait()
    text = q.shape[0]
    heads = q.shape[1] // HD
    kv_heads = kvc // HD
    group = heads // kv_heads
    cols = group * text
    live = (
        lax.rem(lax.broadcasted_iota(jnp.int32, (1, cols), 1), text) < len_ref[0]
    ).astype(F32)
    valid = lax.broadcasted_iota(jnp.int32, (srows, 1), 0) < tiles_ref[0] * (srows // TILES)
    for h in range(kv_heads):
        qs = jnp.concatenate(
            [q[:, (h * group + r) * HD : (h * group + r + 1) * HD] for r in range(group)], axis=0
        )
        cs = jnp.concatenate(
            [c[:, (h * group + r) * HD : (h * group + r + 1) * HD] for r in range(group)], axis=0
        )
        keys = kv[:, h * HD : (h + 1) * HD]
        vals = kv[:, kvc + h * HD : kvc + (h + 1) * HD]
        scores = jnp.where(valid, dot(keys, qs, NT) * HD ** (-0.5), -1e30)
        shifted = jnp.exp(scores - jnp.max(scores, axis=0, keepdims=True))
        att = shifted / jnp.sum(shifted, axis=0, keepdims=True)
        kept = (att.astype(BF16).astype(F32) * live).astype(BF16)
        dp = dot(vals, cs, NT)
        delta = jnp.sum(att * dp, axis=0, keepdims=True)
        ds = (att * (dp - delta) * live * HD ** (-0.5)).astype(BF16)
        dkv_own[:, h * HD : (h + 1) * HD] = dot(ds, qs, NN).astype(BF16)
        dkv_own[:, kvc + h * HD : kvc + (h + 1) * HD] = dot(kept, cs, NN).astype(BF16)

    dkv_c = [send(dkv_own, dkv.at[d], (s, to, m)) for to in samples]
    own = dkv_own[...]
    dkv[d] = own
    back_p[...] = ADAPTER_SCALE * (dot(own[:, :kvc], ukk, NT) + dot(own[:, kvc:], uvv, NT))
    back_c = [
        send(back_p, back_r.at[d, m], (s, lax.rem(d + i, D), lax.rem(m + j, M)))
        for i, j in others
    ]
    back_r[d, m] = back_p[...]
    for copy in dkv_c:
        copy.wait_recv()
    dall = dkv[...].reshape(rows, 2 * kvc)

    step = min(cw, 1024)
    for j in range(0, cw, step):
        g[:, :, j : j + step] = dot(dall, w[j : j + step, :], NT).reshape(nb, rows_loc, step)

    for copy in back_c:
        copy.wait_recv()
    back = jnp.sum(back_r[...], axis=1).reshape(rows, back_r.shape[3]).astype(BF16)

    if cw >= qw:
        @pl.when(lax.div(m, cw // qw) == d)
        def _():
            at = columns(lax.rem(m, cw // qw) * qw, qw)
            g[:, :, at] = g[:, :, at] + dot(back, a[...], NT).reshape(nb, rows_loc, qw)
    else:
        @pl.when(lax.div(d, qw // cw) == m)
        def _():
            at = columns(lax.rem(d, qw // cw) * cw, cw)
            g[...] = g[...] + dot(back, a[at, :], NT).reshape(nb, rows_loc, cw)

    def adapter_up():
        for copy in lowb_c:
            copy.wait_recv()
        low = low_b[...].reshape(rows, low_b.shape[2])
        rank = low.shape[1] // 2
        gup_ref[0] = (ADAPTER_SCALE * dot(low, dall[:, :kvc], TN)[:rank]).astype(BF16)
        gup_ref[1] = (ADAPTER_SCALE * dot(low, dall[:, kvc:], TN)[rank:]).astype(BF16)
        store(gup_ref, gup_hbm)

    def adapter_down():
        for copy in xq_c:
            copy.wait_recv()
        all_q = xq[...].astype(F32).reshape(rows, qw).astype(BF16)
        gdown_ref[...] = dot(all_q, back, TN).astype(BF16)
        store(gdown_ref, gdown_hbm)

    ladder = list(reversed(s_bits))
    flying = {}

    def halve_send(n, p):
        b = ladder[n]
        count = S // (2 * b)
        theirs = lax.rem(s, b) + b * (1 - lax.rem(lax.div(s, b), 2))
        for i in range(D):
            for t in range(count):
                halves[2 * n][p, i * count + t] = g[
                    i * S + theirs + 2 * b * t, :, p * pw : (p + 1) * pw
                ].astype(BF16)
        flying[p] = [send(halves[2 * n].at[p], halves[2 * n + 1].at[p], (flip(s, b), d, m))]

    def halve_take(n, p):
        b = ladder[n]
        count = S // (2 * b)
        ours = lax.rem(s, b) + b * lax.rem(lax.div(s, b), 2)
        flying[p][0].wait_recv()
        for i in range(D):
            for t in range(count):
                at = i * S + ours + 2 * b * t
                g[at, :, p * pw : (p + 1) * pw] = g[at, :, p * pw : (p + 1) * pw] + halves[
                    2 * n + 1
                ][p, i * count + t].astype(F32)

    def group_send(p):
        for j in range(1, M):
            to = lax.rem(m + j, M)
            for i in range(D):
                zs[p, j - 1, i] = g[i * S + s, :, columns(p * pw + to * zw, zw)].astype(BF16)
        flying[p] = [
            send(zs.at[p, j - 1], zr.at[p, j - 1], (s, d, lax.rem(m + j, M)))
            for j in range(1, M)
        ]

    def group_take(p):
        for copy in flying[p]:
            copy.wait_recv()
        for i in range(D):
            total = g[i * S + s, :, columns(p * pw + m * zw, zw)]
            for j in range(M - 1):
                total = total + zr[p, j, i].astype(F32)
            fin[p, i] = total.astype(BF16)
        flying[p] = []
        for i, j in others:
            to = lax.rem(d + i, D)
            flying[p].append(
                send(fin.at[p, to], fr.at[p, d * M + m], (s, to, lax.rem(m + j, M)))
            )
        fr[p, d * M + m] = fin[p, d]

    stores = []

    def store(src, dst):
        copy = pltpu.make_async_copy(src, dst, store_sem.at[len(stores)])
        copy.start()
        stores.append(copy)

    def finish(p):
        for copy in flying[p]:
            copy.wait_recv()
        store(fr.at[p], gimg_hbm.at[p])

    for p in range(parts):
        halve_send(0, p)
    stages = []
    for n in range(1, len(ladder)):
        stages.append(lambda p, n=n: (halve_take(n - 1, p), halve_send(n, p)))
    stages.append(lambda p: (halve_take(len(ladder) - 1, p), group_send(p)))
    stages.append(group_take)
    stages.append(finish)
    for t in range(parts + len(stages) - 1):
        for k, stage in enumerate(stages):
            if k == len(stages) - 1 and t == parts + k - 2:
                adapter_down()
            if 0 <= t - k < parts:
                stage(t - k)
            if k == 0 and t == min(1, parts - 1):
                adapter_up()
    for copy in stores:
        copy.wait()
    for copy in started:
        copy.wait_send()


def deliver(sizes, parts, x0, x1, x2, y0, y1, y2, wide, sems):
    D, M = sizes
    zw = x2.shape[3]
    copies = [
        pltpu.make_async_copy(x, y, sems.at[i])
        for i, (x, y) in enumerate([(x0, y0), (x1, y1), (wide, y2)])
    ]
    copies[0].start()
    copies[1].start()
    for i in range(D):
        for p in range(parts):
            for j in range(M):
                at = ((i * parts + p) * M + j) * zw
                wide[:, at : at + zw] = x2[p, i * M + j].astype(F32)
    copies[2].start()
    for copy in copies:
        copy.wait()


def body(
    encoder_image_states,
    frozen_key_value,
    adapter_down_weight,
    adapter_up_weight,
    queries,
    cotangent,
    text_token_length,
    image_tile_count,
    *,
    sizes,
):
    S, D, M = sizes
    rows_loc, width = encoder_image_states.shape[1:]
    cw, kvc = frozen_key_value.shape[1], frozen_key_value.shape[3]
    qw, ranks = adapter_down_weight.shape[1:]
    text, qcols = queries.shape[2:]
    nb = S * D
    rows, srows = nb * rows_loc, S * rows_loc
    parts = max(1, min(2, cw // M // 128))
    pw = cw // parts
    zw = pw // M
    vmem = pl.BlockSpec(memory_space=pltpu.VMEM)
    smem = pl.BlockSpec(memory_space=pltpu.SMEM)
    hbm = pl.BlockSpec(memory_space=pl.ANY)
    halves = []
    bits = bits_down(S)
    for b in reversed(bits):
        halves += [pltpu.VMEM((parts, D * S // (2 * b), rows_loc, pw), BF16)] * 2
    sends = (nb - 1) + (S - 1) + (M - 1) + 5 * (D - 1) + (D * M - 1)
    sends += parts * (len(bits) + (M - 1) + (D * M - 1))
    shapes = (
        jax.ShapeDtypeStruct((qw, ranks), BF16),
        jax.ShapeDtypeStruct(adapter_up_weight.shape[1:], BF16),
        jax.ShapeDtypeStruct((rows_loc, width), F32),
    )
    down, up, image = pl.pallas_call(
        functools.partial(kernel, sizes, parts),
        out_shape=(*shapes[:2], jax.ShapeDtypeStruct((parts, D * M, rows_loc, zw), BF16)),
        in_specs=[smem, smem] + [hbm] * 6,
        out_specs=(hbm, hbm, hbm),
        scratch_shapes=[
            pltpu.VMEM(adapter_up_weight.shape[1:], BF16),
            pltpu.VMEM((qw, ranks), BF16),
            pltpu.VMEM(adapter_up_weight.shape[1:], BF16),
            pltpu.VMEM((kvc // HD, cw, 2, HD), BF16),
            pltpu.VMEM((cw, 2 * kvc), BF16),
            pltpu.VMEM((qw, ranks), BF16),
            pltpu.VMEM((text, qcols), BF16),
            pltpu.VMEM((text, qcols), BF16),
            pltpu.VMEM((nb, rows_loc, cw), BF16),
            pltpu.VMEM((D, S, rows_loc, qw), BF16),
            pltpu.VMEM((srows, ranks), F32),
            pltpu.VMEM((M, srows, ranks), F32),
            pltpu.VMEM((D, srows, ranks), BF16),
            pltpu.VMEM((2, D, srows, kvc), F32),
            pltpu.VMEM((2, D, srows, kvc), F32),
            pltpu.VMEM((srows, 2 * kvc), BF16),
            pltpu.VMEM((D, srows, 2 * kvc), BF16),
            pltpu.VMEM((srows, ranks), F32),
            pltpu.VMEM((D, M, srows, ranks), F32),
            pltpu.VMEM((nb, rows_loc, cw), F32),
            pltpu.VMEM((parts, M - 1, D, rows_loc, zw), BF16),
            pltpu.VMEM((parts, M - 1, D, rows_loc, zw), BF16),
            pltpu.VMEM((parts, D, rows_loc, zw), BF16),
            pltpu.VMEM((parts, D * M, rows_loc, zw), BF16),
            pltpu.SemaphoreType.DMA((6 + kvc // HD,)),
            pltpu.SemaphoreType.DMA((2 + parts,)),
            pltpu.SemaphoreType.DMA((sends,)),
            pltpu.SemaphoreType.DMA((sends,)),
            *halves,
        ],
        compiler_params=pltpu.CompilerParams(
            collective_id=0, has_side_effects=True, vmem_limit_bytes=58 * 2**20
        ),
    )(
        text_token_length,
        image_tile_count,
        encoder_image_states[0],
        adapter_up_weight[0],
        frozen_key_value[0],
        adapter_down_weight[0],
        queries[0, 0],
        cotangent[0, 0],
    )
    down, up, image = pl.pallas_call(
        functools.partial(deliver, (D, M), parts),
        out_shape=shapes,
        in_specs=[vmem] * 3,
        out_specs=(hbm,) * 3,
        scratch_shapes=[pltpu.VMEM((rows_loc, width), F32), pltpu.SemaphoreType.DMA((3,))],
    )(down, up, image)
    return down[None], up[None], image[None]


def solution(mesh):
    in_specs = (
        P("dp", "segment", None),
        P("segment", "dp", None, "mp"),
        P("segment", "mp", None),
        P("segment", None, None, "mp"),
        P("segment", "dp", None, "mp"),
        P("segment", "dp", None, "mp"),
        P("dp"),
        P("dp"),
    )
    out_specs = (P("segment", "mp", None), P("segment", None, None, "mp"), P("dp", "segment", None))
    sizes = (mesh.shape["segment"], mesh.shape["dp"], mesh.shape["mp"])
    return jax.shard_map(
        functools.partial(body, sizes=sizes),
        mesh=mesh, in_specs=in_specs, out_specs=out_specs, check_vma=False,
    )
```
